256 devices in a mesh: seq: 32 (over x, z_lo, core), batch: 8 (over y, z_hi).
Axes of the slice: x: 4, y: 4, z: 8 (z_hi: 2, z_lo: 4; z = z_hi * 4 + z_lo), core: 2. Of those that a mesh axis runs over, the one named last changes fastest.
Arguments:
- hidden: bfloat16 [8, 32, 448, 1152], P('batch', 'seq'), may hold values from -6 to 6
- modulation: float32 [8, 2, 3, 1152], P('batch'), may hold values from -3 to 3
- w_qkv: bfloat16 [2, 1152, 3456], P(None, 'seq'), may hold values from -6 to 6
- w_out: bfloat16 [2, 1152, 1152], P(None, 'seq'), may hold values from -0.1875 to 0.1875
Outputs:
- hidden_out: bfloat16 [8, 32, 448, 1152], P('batch', 'seq')
- guided: bfloat16 [8, 32, 448, 1152], P('batch', 'seq')
The draws below stay inside these ranges and needn't reach their ends.
All inputs are finite; a program needn't handle non-finite values.
Results may differ from the reference program's by a relative error of at most 0.017.
Values may be sent and summed in bfloat16 or wider, within the bound.
No kernel may reach another device: no remote copies, remote signals or barrier semaphores. Data moves between devices by JAX's collectives and lax.ppermute only.
A program may use at most 128 MiB of HBM per device.

```python
import jax
import jax.numpy as jnp
from jax import lax

D = 1152
HEADS = 16
HEAD_DIM = 72
PATCHES = 448
FRAMES = 32
SAMPLES = 8


def draw_w_qkv(key, part):
    key = jax.random.fold_in(key, 11)
    shape = (2, D, 3 * D)
    values = jax.random.truncated_normal(key, -4.0, 4.0, shape, jnp.float32)
    return (values * D ** (-0.5)).astype(jnp.bfloat16)


def steps_of(rng, extent, cuts, low, high):
    loudness = 1.0
    for dim, blocks in cuts:
        draws = jax.random.uniform(jax.random.fold_in(jax.random.fold_in(rng, 6), dim), (blocks,), jnp.float32, low / len(cuts), high / len(cuts))
        loudness = loudness * jnp.repeat(jnp.exp(draws), extent[dim] // blocks).reshape((-1,) + (1,) * (len(extent) - 1 - dim))
    return loudness


def scatter_about(key, extent, scale, bound, split=(), kind=jnp.bfloat16):
    factor_of = steps_of(key, extent, split, -0.22, 0.18) if split else 1.0
    entries = jax.random.normal(key, extent, jnp.float32) * scale * factor_of
    return jnp.minimum(jnp.maximum(entries, -bound), bound).astype(kind)


def setup_inputs(seed: int = 0) -> dict:
    splits = jax.random.split(jax.random.key(seed), 5)
    return {
        "hidden": scatter_about(splits[0], (SAMPLES, FRAMES, PATCHES, D), 1.0, 6.0, ((0, 8), (1, 32))),
        "modulation": scatter_about(splits[1], (SAMPLES, 2, 3, D), 0.7, 3.0, ((0, 8),), jnp.float32),
        "w_qkv": draw_w_qkv(jax.random.fold_in(splits[4], 71), 0),
        "w_out": scatter_about(splits[3], (2, D, D), D ** -0.5, 0.1875, ((1, 32),)),
    }


def normalize(state, shift, scale):
    mean = lax.optimization_barrier(jnp.mean(state, axis=-1, keepdims=True))
    centered = state - mean
    spread = lax.optimization_barrier(jnp.mean(centered * centered, axis=-1, keepdims=True))
    return (centered * lax.rsqrt(spread + 1e-06) * (1.0 + scale) + shift).astype(jnp.bfloat16)

def attend_group(query_rows, key_tile, value_tile):
    logit_scores = jnp.einsum('bxu,sxu->xbs', query_rows.astype(jnp.float32), key_tile.astype(jnp.float32))
    logit_scores = logit_scores * HEAD_DIM ** (-0.5)
    attention_probabilities = jax.nn.softmax(logit_scores, axis=-1).astype(jnp.bfloat16)
    attention_result = jnp.einsum('zjc,czx->jzx', attention_probabilities.astype(jnp.float32), value_tile.astype(jnp.float32))
    return attention_result.astype(jnp.bfloat16)

def one_sample(operands, w_qkv, w_out):
    video, mods = operands
    state = video.astype(jnp.float32)
    normed = normalize(state, mods[0, 0], mods[0, 1]).reshape(FRAMES * PATCHES, D)
    joined = jnp.dot(normed, w_qkv[0], preferred_element_type=jnp.float32).astype(jnp.bfloat16)
    joined = joined.reshape(FRAMES, PATCHES, 3, HEADS, HEAD_DIM)
    attended = lax.map(lambda block: attend_group(block[:, 0], block[:, 1], block[:, 2]), joined)
    attended = attended.reshape(FRAMES * PATCHES, D)
    projected = jnp.dot(attended, w_out[0], preferred_element_type=jnp.float32).reshape(FRAMES, PATCHES, D)
    layer_one = (state + mods[0, 2] * projected).astype(jnp.bfloat16)
    state = layer_one.astype(jnp.float32)
    normed = normalize(state, mods[1, 0], mods[1, 1]).reshape(FRAMES * PATCHES, D)
    joined = jnp.dot(normed, w_qkv[1], preferred_element_type=jnp.float32).astype(jnp.bfloat16)
    joined = jnp.transpose(joined.reshape(FRAMES, PATCHES, 3, HEADS, HEAD_DIM), (1, 0, 2, 3, 4))
    attended = jax.vmap(lambda block: attend_group(block[:, 0], block[:, 1], block[:, 2]))(joined)
    attended = jnp.transpose(attended, (1, 0, 2, 3)).reshape(FRAMES * PATCHES, D)
    projected = jnp.dot(attended, w_out[1], preferred_element_type=jnp.float32).reshape(FRAMES, PATCHES, D)
    return (state + mods[1, 2] * projected).astype(jnp.bfloat16)

def reference(hidden, modulation, w_qkv, w_out):
    hidden_out = lax.map(lambda pair: one_sample(pair, w_qkv, w_out), (hidden, modulation))
    paired = hidden_out.astype(jnp.float32).reshape(SAMPLES // 2, 2, FRAMES, PATCHES, D)
    cond_part = paired[:, 0]
    unguided_portion = paired[:, 1]
    combined = (unguided_portion + 3.0 * (cond_part - unguided_portion)).astype(jnp.bfloat16)
    guided = jnp.repeat(combined, 2, axis=0)
    return (hidden_out, guided)
```

```python
import jax
import jax.numpy as jnp
from jax import lax
from jax.experimental import pallas as pl
from jax.experimental.pallas import tpu as pltpu
from jax.sharding import Mesh, PartitionSpec as P

HEADS = 16
SIZE = 72
WIDTH = HEADS * SIZE
SHARD = 36
PADDED = 40
SHARDS = WIDTH // SHARD
DEEP = SHARDS * PADDED
COLUMNS = 4 * WIDTH
WINDOW = 256
PATCHES = 448
ROWS = 512
EXPONENT = SIZE**-0.5 * 1.4426950408889634
SEQ = ("x", "zl", "c")
PAIRED = ("zh", "x", "zl", "c")


def normalize(state, shift, scale):
    mean = jnp.mean(state, axis=-1, keepdims=True)
    centered = state - mean
    spread = jnp.mean(centered * centered, axis=-1, keepdims=True)
    return (centered * lax.rsqrt(spread + 1e-06) * (1.0 + scale) + shift).astype(jnp.bfloat16)


def spread_matrix():
    source = lax.broadcasted_iota(jnp.int32, (WIDTH, 1), 0)
    target = source + (PADDED - SHARD) * (source // SHARD)
    place = lax.broadcasted_iota(jnp.int32, (WIDTH, DEEP), 1)
    return jnp.where(place == target, 1.0, 0.0).astype(jnp.bfloat16)


def spread_columns(block, matrix):
    return jnp.dot(block, matrix, preferred_element_type=jnp.float32).astype(jnp.bfloat16)


def project_in(normed, w_ref, qkv_ref, step=384):
    for first in range(0, 3 * WIDTH, step):
        part = jnp.dot(normed, w_ref[:, first : first + step], preferred_element_type=jnp.float32)
        qkv_ref[:, first : first + step] = part.astype(jnp.bfloat16)


def attend(qkv_ref, total_ref, low, count, allowed):
    rows = pl.ds(low, count)
    lane = lax.broadcasted_iota(jnp.int32, (1, WINDOW), 1)
    for head in range(HEADS):
        start = min(head * SIZE // 128 * 128, WIDTH - WINDOW)
        inner = head * SIZE - start
        spare = 0 if inner > 0 else WINDOW - 1
        mine = jnp.where((lane >= inner) & (lane < inner + SIZE), 1.0, 0.0)
        mask = mine.astype(jnp.bfloat16)
        unit = jnp.where(lane == spare, 1.0, 0.0).astype(jnp.bfloat16)
        query = qkv_ref[rows, start : start + WINDOW] * mask
        key = qkv_ref[rows, WIDTH + start : WIDTH + start + WINDOW]
        value = qkv_ref[rows, 2 * WIDTH + start : 2 * WIDTH + start + WINDOW] * mask + unit
        scores = lax.dot_general(
            query, key, (((1,), (1,)), ((), ())), preferred_element_type=jnp.float32
        )
        if allowed is not None:
            scores = jnp.where(allowed, scores, -jnp.inf)
        top = jnp.max(scores, axis=1, keepdims=True)
        weights = jnp.exp2((scores - top) * EXPONENT).astype(jnp.bfloat16)
        result = jnp.dot(weights, value, preferred_element_type=jnp.float32)
        factor = 1.0 / result[:, spare : spare + 1]
        part = result * factor * mine
        columns = pl.ds(start, WINDOW)
        total_ref[rows, columns] = total_ref[rows, columns] + part


def project_out(total_ref, matrix, w_ref):
    attended = spread_columns(total_ref[...].astype(jnp.bfloat16), matrix)
    return jnp.dot(attended, w_ref[:, 3 * WIDTH :], preferred_element_type=jnp.float32)


def prepare_kernel(x_ref, mods_ref, out_ref):
    normed = normalize(x_ref[...].astype(jnp.float32), mods_ref[0:1, :], mods_ref[1:2, :])
    out_ref[...] = spread_columns(normed, spread_matrix())


def spatial_kernel(normed_ref, x_ref, mods_ref, w_ref, out_ref, qkv_ref, total_ref):
    project_in(normed_ref[...], w_ref, qkv_ref)
    total_ref[...] = jnp.zeros_like(total_ref)
    attend(qkv_ref, total_ref, 0, PATCHES, None)
    projected = project_out(total_ref, spread_matrix(), w_ref)
    state = x_ref[...].astype(jnp.float32) + mods_ref[2:3, :] * projected
    out_ref[0:PATCHES, :] = state.astype(jnp.bfloat16)
    out_ref[PATCHES:, :] = jnp.zeros((ROWS - PATCHES, WIDTH), jnp.bfloat16)


def temporal_kernel(x_ref, mods_ref, w_ref, out_ref, normed_ref, qkv_ref, total_ref):
    half = ROWS // 2
    matrix = spread_matrix()
    for sample in range(2):
        state = x_ref[sample * half : (sample + 1) * half, :].astype(jnp.float32)
        normed = normalize(state, mods_ref[sample, 0:1, :], mods_ref[sample, 1:2, :])
        normed_ref[sample * half : (sample + 1) * half, :] = spread_columns(normed, matrix)
    project_in(normed_ref[...], w_ref, qkv_ref)
    total_ref[...] = jnp.zeros_like(total_ref)
    row = lax.broadcasted_iota(jnp.int32, (half, half), 0)
    column = lax.broadcasted_iota(jnp.int32, (half, half), 1)
    allowed = (row & 7) == (column & 7)
    for sample in range(2):
        attend(qkv_ref, total_ref, sample * half, half, allowed)
    projected = project_out(total_ref, matrix, w_ref)
    results = []
    for sample in range(2):
        state = x_ref[sample * half : (sample + 1) * half, :].astype(jnp.float32)
        state = state + mods_ref[sample, 2:3, :] * projected[sample * half : (sample + 1) * half]
        results.append(state.astype(jnp.bfloat16).astype(jnp.float32))
    cond, uncond = results
    guided = (uncond + 3.0 * (cond - uncond)).reshape(32, 8, WIDTH)
    for sample in range(2):
        both = jnp.concatenate([results[sample].reshape(32, 8, WIDTH), guided], axis=1)
        out_ref[sample * 32 : (sample + 1) * 32] = both.astype(jnp.bfloat16)


def kernel_call(body, out_shape, scratch, flops, moved):
    return pl.pallas_call(
        body,
        out_shape=jax.ShapeDtypeStruct(out_shape, jnp.bfloat16),
        scratch_shapes=scratch,
        cost_estimate=pl.CostEstimate(flops=flops, bytes_accessed=moved, transcendentals=0),
        compiler_params=pltpu.CompilerParams(vmem_limit_bytes=56 * 2**20),
    )


def on_device(hidden, modulation, w_qkv, w_out):
    state = hidden.reshape(PATCHES, WIDTH)
    mods = modulation[0]

    def gathered(layer):
        joined = jnp.concatenate([w_qkv[layer], w_out[layer]], axis=1)
        joined = jnp.pad(joined, ((0, PADDED - SHARD), (0, 0)))
        return lax.all_gather(joined, SEQ, axis=0, tiled=False).reshape(DEEP, COLUMNS)

    weights = [gathered(0), gathered(1)]
    other = lax.ppermute(mods[1], "zh", [(0, 1), (1, 0)])
    first = lax.axis_index("zh") == 0
    both_mods = jnp.stack([jnp.where(first, mods[1], other), jnp.where(first, other, mods[1])])

    normed = kernel_call(prepare_kernel, (PATCHES, DEEP), [], 10**9, 10**7)(state, mods[0])
    layer_one = kernel_call(
        spatial_kernel,
        (ROWS, WIDTH),
        [pltpu.VMEM((PATCHES, 3 * WIDTH), jnp.bfloat16), pltpu.VMEM((PATCHES, WIDTH), jnp.float32)],
        10**10,
        2 * 10**7,
    )(normed, state, mods[0], weights[0])
    by_patch = lax.all_to_all(layer_one.reshape(64, 8, WIDTH), PAIRED, 0, 0, tiled=True)
    result = kernel_call(
        temporal_kernel,
        (64, 16, WIDTH),
        [
            pltpu.VMEM((ROWS, DEEP), jnp.bfloat16),
            pltpu.VMEM((ROWS, 3 * WIDTH), jnp.bfloat16),
            pltpu.VMEM((ROWS, WIDTH), jnp.float32),
        ],
        10**10,
        2 * 10**7,
    )(by_patch.reshape(ROWS, WIDTH), both_mods, weights[1])
    by_frame = lax.all_to_all(result, PAIRED, 0, 0, tiled=True)
    hidden_out = by_frame[:, :8].reshape(ROWS, WIDTH)[:PATCHES]
    guided = by_frame[:, 8:].reshape(ROWS, WIDTH)[:PATCHES]
    return hidden_out.reshape(hidden.shape), guided.reshape(hidden.shape)


def solution(mesh):
    split = Mesh(mesh.devices.reshape(4, 4, 2, 4, 2), ("x", "zl", "c", "y", "zh"))
    batch, seq = ("y", "zh"), SEQ
    placed = (
        P(batch, seq, None, None),
        P(batch, None, None, None),
        P(None, seq, None),
        P(None, seq, None),
    )
    return jax.shard_map(
        on_device,
        mesh=split,
        in_specs=placed,
        out_specs=(P(batch, seq, None, None), P(batch, seq, None, None)),
        check_vma=False,
    )
```

```python
import jax
import jax.numpy as jnp
from jax import lax
from jax.experimental import pallas as pl
from jax.experimental.pallas import tpu as pltpu
from jax.sharding import Mesh, PartitionSpec as P

HEADS = 16
SIZE = 72
WIDTH = HEADS * SIZE
SHARD = 36
WINDOW = 256
PATCHES = 448
ROWS = 512
EXPONENT = SIZE**-0.5 * 1.4426950408889634
SEQ = ("x", "zl", "c")
PAIRED = ("zh", "x", "zl", "c")
BLOCK = 4 * SHARD
PAIR = 2 * WIDTH
LEFT = 640
RIGHT = WIDTH - LEFT
FIRST = PAIR + LEFT
START = 4 * LEFT
CUT = 1536


def normalize(state, shift, scale):
    mean = jnp.mean(state, axis=-1, keepdims=True)
    centered = state - mean
    spread = jnp.mean(centered * centered, axis=-1, keepdims=True)
    return (centered * lax.rsqrt(spread + 1e-06) * (1.0 + scale) + shift).astype(jnp.bfloat16)


def order_matrix(by_x):
    feature = lax.broadcasted_iota(jnp.int32, (WIDTH, 1), 0)
    x, zl, c, row = feature // 288, (feature // 72) & 3, (feature // 36) & 1, feature % SHARD
    if by_x:
        place = (zl * 2 + c) * 4 + ((x - lax.axis_index("x")) & 3)
    else:
        place = (x * 2 + c) * 4 + ((zl - lax.axis_index("zl")) & 3)
    column = lax.broadcasted_iota(jnp.int32, (WIDTH, WIDTH), 1)
    return jnp.where(column == place * SHARD + row, 1.0, 0.0).astype(jnp.bfloat16)


def spread_columns(block, matrix):
    return jnp.dot(block, matrix, preferred_element_type=jnp.float32).astype(jnp.bfloat16)


def attend(qkv_ref, total_ref, groups, allowed):
    rows = qkv_ref.shape[0] // groups
    lane = lax.broadcasted_iota(jnp.int32, (1, 1, WINDOW), 2)
    for head in range(HEADS):
        start = min(head * SIZE // 128 * 128, WIDTH - WINDOW)
        inner = head * SIZE - start
        spare = 0 if inner > 0 else WINDOW - 1
        mine = jnp.where((lane >= inner) & (lane < inner + SIZE), 1.0, 0.0)
        mask = mine.astype(jnp.bfloat16)
        unit = jnp.where(lane == spare, 1.0, 0.0).astype(jnp.bfloat16)

        def window(first):
            return qkv_ref[:, first + start : first + start + WINDOW].reshape(groups, rows, WINDOW)

        query, key, value = window(0) * mask, window(WIDTH), window(2 * WIDTH) * mask + unit
        scores = lax.dot_general(
            query, key, (((2,), (2,)), ((0,), (0,))), preferred_element_type=jnp.float32
        )
        if allowed is not None:
            scores = jnp.where(allowed, scores, -jnp.inf)
        top = jnp.max(scores, axis=2, keepdims=True)
        weights = jnp.exp2((scores - top) * EXPONENT).astype(jnp.bfloat16)
        result = lax.dot_general(
            weights, value, (((2,), (1,)), ((0,), (0,))), preferred_element_type=jnp.float32
        )
        factor = 1.0 / result[:, :, spare : spare + 1]
        part = (result * factor * mine).reshape(groups * rows, WINDOW)
        columns = pl.ds(start, WINDOW)
        total_ref[:, columns] = total_ref[:, columns] + part


def prepare_kernel(x_ref, mods_ref, first_ref, second_ref, by_x_ref, by_z_ref):
    normed = normalize(x_ref[...].astype(jnp.float32), mods_ref[0:1, :], mods_ref[1:2, :])
    for out_ref, matrix_ref, by_x in ((first_ref, by_x_ref, True), (second_ref, by_z_ref, False)):
        matrix_ref[...] = order_matrix(by_x)
        out_ref[...] = spread_columns(normed, matrix_ref[...])


def spatial_kernel(first_ref, second_ref, matrix_ref, x_ref, mods_ref, *refs):
    blocks, (out_ref, w_first, w_second, qkv_ref, total_ref, sems) = refs[:18], refs[18:]
    x, zl, c = (lax.axis_index(name) for name in SEQ)
    copies = []

    def bring(target, source, index, low=0, count=PAIR):
        rows = pl.ds(pl.multiple_of(index * BLOCK, BLOCK), BLOCK)
        target = target.at[rows, low : low + count]
        copies.append(pltpu.make_async_copy(source.at[:, :count], target, sems.at[len(copies)]))
        copies[-1].start()

    for side in range(2):
        own, up, down, far_up, far_down = blocks[9 * side : 9 * side + 5]
        core = c ^ side
        bring(w_first, own, zl * 2 + core)
        bring(w_first, up, ((zl + 3) & 3) * 2 + core)
        bring(w_first, down, ((zl + 1) & 3) * 2 + core)
        bring(w_first, far_up, ((zl + 2) & 3) * 2 + core, 0, CUT)
        bring(w_first, far_down, ((zl + 2) & 3) * 2 + core, CUT, PAIR - CUT)
    for side in range(2):
        core = c ^ side
        for block, apart in zip(blocks[9 * side + 5 : 9 * side + 9], (0, 3, 1, 2)):
            bring(w_second, block, ((x + apart) & 3) * 2 + core)
    total_ref[...] = jnp.zeros_like(total_ref)
    for copy in copies[:10]:
        copy.wait()
    for low in range(0, PAIR, 384):
        part = jnp.dot(first_ref[...], w_first[:, low : low + 384], preferred_element_type=jnp.float32)
        qkv_ref[:, low : low + 384] = part.astype(jnp.bfloat16)
    for copy in copies[10:]:
        copy.wait()
    for low in range(0, WIDTH, 384):
        part = jnp.dot(second_ref[...], w_second[:, low : low + 384], preferred_element_type=jnp.float32)
        qkv_ref[:, PAIR + low : PAIR + low + 384] = part.astype(jnp.bfloat16)
    attend(qkv_ref, total_ref, 1, None)
    attended = spread_columns(total_ref[...].astype(jnp.bfloat16), matrix_ref[...])
    projected = jnp.dot(attended, w_second[:, WIDTH:], preferred_element_type=jnp.float32)
    state = x_ref[...].astype(jnp.float32) + mods_ref[2:3, :] * projected
    out_ref[0:PATCHES, :] = state.astype(jnp.bfloat16)
    out_ref[PATCHES:, :] = jnp.zeros((ROWS - PATCHES, WIDTH), jnp.bfloat16)


def temporal_kernel(x_ref, mods_ref, *refs):
    blocks, parts, others, orders = refs[:18], refs[18:21], refs[21:24], refs[24:26]
    out_ref, w_first, w_second, order_ref, first_ref, second_ref, qkv_ref, total_ref, sems = refs[26:]
    half = ROWS // 2
    x, zl, c = (lax.axis_index(name) for name in SEQ)
    turn = lax.axis_index("y")
    copies = []

    def bring(source, target):
        copies.append(pltpu.make_async_copy(source, target, sems.at[len(copies)]))
        copies[-1].start()

    def rows(index):
        return pl.ds(pl.multiple_of(index * BLOCK, BLOCK), BLOCK)

    for index in range(2):
        bring(orders[index], order_ref.at[index])
    for side in range(2):
        core = c ^ side
        mine = blocks[9 * side : 9 * side + 9]
        for piece, low, apart in zip(mine[:3] + mine[4:5], (PAIR,) * 3 + (PAIR - CUT,), (0, 3, 1, 2)):
            target = w_first.at[turn, rows(((zl + apart) & 3) * 2 + core)]
            bring(piece.at[:, low : low + LEFT], target)
        for piece, apart in zip(mine[5:], (0, 3, 1, 2)):
            target = w_second.at[turn, rows(((x + apart) & 3) * 2 + core)]
            bring(piece.at[:, PAIR : PAIR + RIGHT], target)
        for part, back in zip((parts, others)[side], (3, 1, 2)):
            owner = (turn + back) & 3
            for index, apart in enumerate((0, 3, 1, 2)):
                piece = part.at[index * BLOCK : (index + 1) * BLOCK]
                target = w_first.at[owner, rows(((zl + apart) & 3) * 2 + core)]
                bring(piece.at[:, :LEFT], target)
                target = w_second.at[owner, rows(((x + apart) & 3) * 2 + core)]
                bring(piece.at[:, LEFT:], target)
    total_ref[...] = jnp.zeros_like(total_ref)
    row = lax.broadcasted_iota(jnp.int32, (half, half), 0)
    column = lax.broadcasted_iota(jnp.int32, (half, half), 1)
    to_patches = jnp.where(column == (row & 31) * 8 + (row >> 5), 1.0, 0.0).astype(jnp.bfloat16)
    to_frames = jnp.where(column == (row & 7) * 32 + (row >> 3), 1.0, 0.0).astype(jnp.bfloat16)
    for copy in copies[:2]:
        copy.wait()
    for sample in range(2):
        state = x_ref[sample * half : (sample + 1) * half, :].astype(jnp.float32)
        normed = normalize(state, mods_ref[sample, 0:1, :], mods_ref[sample, 1:2, :])
        normed = spread_columns(to_patches, normed)
        for index, target in enumerate((first_ref, second_ref)):
            target[sample * half : (sample + 1) * half, :] = spread_columns(normed, order_ref[index])
    for copy in copies[2:]:
        copy.wait()
    for index in range(4):
        part = jnp.dot(first_ref[...], w_first[index], preferred_element_type=jnp.float32)
        qkv_ref[:, index * LEFT : (index + 1) * LEFT] = part.astype(jnp.bfloat16)
    for index, count in enumerate((RIGHT, 3 * WIDTH - START - RIGHT)):
        low = START + index * RIGHT
        part = jnp.dot(second_ref[...], w_second[index, :, :count], preferred_element_type=jnp.float32)
        qkv_ref[:, low : low + count] = part.astype(jnp.bfloat16)
    row = lax.broadcasted_iota(jnp.int32, (1, 128, 128), 1)
    column = lax.broadcasted_iota(jnp.int32, (1, 128, 128), 2)
    attend(qkv_ref, total_ref, 4, (row >> 5) == (column >> 5))
    attended = total_ref[...].astype(jnp.bfloat16)
    attended = [
        spread_columns(to_frames, attended[sample * half : (sample + 1) * half]) for sample in range(2)
    ]
    attended = jnp.concatenate(attended, axis=0)
    attended = spread_columns(attended, order_ref[1])
    outward = (w_second[1, :, 3 * WIDTH - START - RIGHT :], w_second[2], w_second[3])
    projected = [jnp.dot(attended, part, preferred_element_type=jnp.float32) for part in outward]
    projected = jnp.concatenate(projected, axis=1)
    results = []
    for sample in range(2):
        state = x_ref[sample * half : (sample + 1) * half, :].astype(jnp.float32)
        state = state + mods_ref[sample, 2:3, :] * projected[sample * half : (sample + 1) * half]
        results.append(state.astype(jnp.bfloat16).astype(jnp.float32))
    cond, uncond = results
    guided = (uncond + 3.0 * (cond - uncond)).reshape(32, 8, WIDTH)
    for sample in range(2):
        both = jnp.concatenate([results[sample].reshape(32, 8, WIDTH), guided], axis=1)
        out_ref[sample * 32 : (sample + 1) * 32] = both.astype(jnp.bfloat16)


def kernel_call(body, out_shape, scratch, flops, moved, specs=None, limit=36):
    return pl.pallas_call(
        body,
        **({} if specs is None else {"in_specs": specs}),
        out_shape=jax.tree.map(
            lambda shape: jax.ShapeDtypeStruct(shape, jnp.bfloat16),
            out_shape,
            is_leaf=lambda shape: isinstance(shape, tuple),
        ),
        scratch_shapes=scratch,
        cost_estimate=pl.CostEstimate(flops=flops, bytes_accessed=moved, transcendentals=0),
        compiler_params=pltpu.CompilerParams(vmem_limit_bytes=limit * 2**20),
    )


def along(block, axis, by):
    return lax.ppermute(block, axis, [(i, (i + by) % 4) for i in range(4)])


def along_z(block, by):
    def index(z):
        return z % 4 * 2 + z // 4

    return lax.ppermute(block, ("zl", "zh"), [(index(z), index((z + by) % 8)) for z in range(8)])


def other_core(block):
    return lax.ppermute(block, "c", [(0, 1), (1, 0)])


def gather_weights(w_qkv, w_out, state, mods):
    turn = lax.axis_index("y")
    later = jnp.concatenate([w_qkv[1], w_out[1]], axis=1)
    later_first = lax.dynamic_slice(later, (0, turn * LEFT), (SHARD, LEFT))
    later_second = lax.dynamic_slice(later, (0, START + turn * RIGHT), (SHARD, RIGHT))
    first = jnp.concatenate([w_qkv[0, :, :PAIR], later_first], axis=1)
    second = jnp.concatenate([w_qkv[0, :, PAIR:], w_out[0], later_second], axis=1)
    up, down, far = along(first, "x", 1), along(first, "x", 3), along(first, "x", 2)
    up_z, down_z = along_z(second, 1), along_z(second, 7)
    far_z = lax.ppermute(second, "zl", [(0, 2), (2, 0), (1, 3), (3, 1)])
    first = jnp.concatenate([first, down, far, up], axis=0)
    second = jnp.concatenate([second, down_z, far_z, up_z], axis=0)
    first, second, state = lax.optimization_barrier((first, second, state))
    near = [along_z(first, 1), along_z(first, 7), along(second, "x", 1), along(second, "x", 3)]
    own_other = [other_core(first), other_core(second)]
    first_far, second_far, near, mods = lax.optimization_barrier((first, second, near, mods))
    far = [along_z(first_far[:, :CUT], 2), along_z(first_far[:, CUT:], 6), along(second_far, "x", 2)]
    near_other = [other_core(block) for block in near]
    mine = [first] + near[:2] + far[:2] + [second] + near[2:] + far[2:]
    left = [block[:, PAIR:] for block in mine[:3]] + [mine[4][:, PAIR - CUT :]]
    right = [block[:, PAIR:] for block in mine[5:]]
    share = jnp.concatenate(
        [jnp.concatenate(left, axis=0), jnp.concatenate(right, axis=0)], axis=1
    )
    other = lax.ppermute(mods, "zh", [(0, 1), (1, 0)])
    leads = lax.axis_index("zh") == 0
    mods = jnp.stack([jnp.where(leads, mods, other), jnp.where(leads, other, mods)])
    share, mods = lax.optimization_barrier((share, mods))
    far_other = [other_core(block) for block in far]
    theirs = own_other[:1] + near_other[:2] + far_other[:2]
    theirs += own_other[1:] + near_other[2:] + far_other[2:]
    parts = [along(share, "y", by) for by in (1, 3, 2)]
    return mine + theirs, parts + [other_core(part) for part in parts], state, mods


def on_device(hidden, modulation, w_qkv, w_out):
    state = hidden.reshape(PATCHES, WIDTH)
    mods = modulation[0]

    weights, later, late_state, both_mods = gather_weights(w_qkv, w_out, state, mods[1])
    shapes = [(PATCHES, WIDTH)] * 2 + [(WIDTH, WIDTH)] * 2
    first, second, by_x, by_z = kernel_call(prepare_kernel, shapes, [], 10**10, 10**7)(late_state, mods[0])
    layer_one = kernel_call(
        spatial_kernel,
        (ROWS, WIDTH),
        [
            pltpu.VMEM((WIDTH, PAIR), jnp.bfloat16),
            pltpu.VMEM((WIDTH, PAIR), jnp.bfloat16),
            pltpu.VMEM((PATCHES, 3 * WIDTH), jnp.bfloat16),
            pltpu.VMEM((PATCHES, WIDTH), jnp.float32),
            pltpu.SemaphoreType.DMA((18,)),
        ],
        10**10,
        2 * 10**7,
        [pl.BlockSpec(memory_space=pltpu.VMEM)] * 5 + [pl.BlockSpec(memory_space=pltpu.HBM)] * 18,
    )(first, second, by_z, state, mods[0], *weights)
    by_patch = lax.all_to_all(layer_one.reshape(64, 8, WIDTH), PAIRED, 0, 0, tiled=True)
    result = kernel_call(
        temporal_kernel,
        (64, 16, WIDTH),
        [
            pltpu.VMEM((4, WIDTH, LEFT), jnp.bfloat16),
            pltpu.VMEM((4, WIDTH, RIGHT), jnp.bfloat16),
            pltpu.VMEM((2, WIDTH, WIDTH), jnp.bfloat16),
            pltpu.VMEM((ROWS, WIDTH), jnp.bfloat16),
            pltpu.VMEM((ROWS, WIDTH), jnp.bfloat16),
            pltpu.VMEM((ROWS, 3 * WIDTH), jnp.bfloat16),
            pltpu.VMEM((ROWS, WIDTH), jnp.float32),
            pltpu.SemaphoreType.DMA((66,)),
        ],
        10**10,
        2 * 10**7,
        [pl.BlockSpec(memory_space=pltpu.VMEM)] * 2 + [pl.BlockSpec(memory_space=pltpu.HBM)] * 26,
        58,
    )(by_patch.reshape(ROWS, WIDTH), both_mods, *weights, *later, by_x, by_z)
    by_frame = lax.all_to_all(result, PAIRED, 0, 0, tiled=True)
    hidden_out = by_frame[:, :8].reshape(ROWS, WIDTH)[:PATCHES]
    guided = by_frame[:, 8:].reshape(ROWS, WIDTH)[:PATCHES]
    return hidden_out.reshape(hidden.shape), guided.reshape(hidden.shape)


def solution(mesh):
    split = Mesh(mesh.devices.reshape(4, 4, 2, 4, 2), ("x", "zl", "c", "y", "zh"))
    batch, seq = ("y", "zh"), SEQ
    placed = (
        P(batch, seq, None, None),
        P(batch, None, None, None),
        P(None, seq, None),
        P(None, seq, None),
    )
    return jax.shard_map(
        on_device,
        mesh=split,
        in_specs=placed,
        out_specs=(P(batch, seq, None, None), P(batch, seq, None, None)),
        check_vma=False,
    )
```

```python
import jax
import jax.numpy as jnp
from jax import lax
from jax.experimental import pallas as pl
from jax.experimental.pallas import tpu as pltpu
from jax.sharding import Mesh, PartitionSpec as P

HEADS = 16
SIZE = 72
WIDTH = HEADS * SIZE
SHARD = 36
WINDOW = 256
PATCHES = 448
ROWS = 512
EXPONENT = SIZE**-0.5 * 1.4426950408889634
SEQ = ("x", "zl", "c")
PAIRED = ("zh", "x", "zl", "c")
BLOCK = 4 * SHARD
PAIR = 2 * WIDTH
LEFT = 640
RIGHT = WIDTH - LEFT
FIRST = PAIR + LEFT
START = 4 * LEFT
CUT = 1536


def normalize(state, shift, scale):
    mean = jnp.mean(state, axis=-1, keepdims=True)
    centered = state - mean
    spread = jnp.mean(centered * centered, axis=-1, keepdims=True)
    return (centered * lax.rsqrt(spread + 1e-06) * (1.0 + scale) + shift).astype(jnp.bfloat16)


def order_matrix(by_x):
    feature = lax.broadcasted_iota(jnp.int32, (WIDTH, 1), 0)
    x, zl, c, row = feature // 288, (feature // 72) & 3, (feature // 36) & 1, feature % SHARD
    if by_x:
        place = (zl * 2 + c) * 4 + ((x - lax.axis_index("x")) & 3)
    else:
        place = (x * 2 + c) * 4 + ((zl - lax.axis_index("zl")) & 3)
    column = lax.broadcasted_iota(jnp.int32, (WIDTH, WIDTH), 1)
    return jnp.where(column == place * SHARD + row, 1.0, 0.0).astype(jnp.bfloat16)


def spread_columns(block, matrix):
    return jnp.dot(block, matrix, preferred_element_type=jnp.float32).astype(jnp.bfloat16)


def attend(qkv_ref, total_ref, groups, allowed):
    rows = qkv_ref.shape[0] // groups
    lane = lax.broadcasted_iota(jnp.int32, (1, 1, WINDOW), 2)
    for head in range(HEADS):
        start = min(head * SIZE // 128 * 128, WIDTH - WINDOW)
        inner = head * SIZE - start
        spare = 0 if inner > 0 else WINDOW - 1
        mine = jnp.where((lane >= inner) & (lane < inner + SIZE), 1.0, 0.0)
        mask = mine.astype(jnp.bfloat16)
        unit = jnp.where(lane == spare, 1.0, 0.0).astype(jnp.bfloat16)

        def window(first):
            return qkv_ref[:, first + start : first + start + WINDOW].reshape(groups, rows, WINDOW)

        query, key, value = window(0) * mask, window(WIDTH), window(2 * WIDTH) * mask + unit
        scores = lax.dot_general(
            query, key, (((2,), (2,)), ((0,), (0,))), preferred_element_type=jnp.float32
        )
        if allowed is not None:
            scores = jnp.where(allowed, scores, -jnp.inf)
        top = jnp.max(scores, axis=2, keepdims=True)
        weights = jnp.exp2((scores - top) * EXPONENT).astype(jnp.bfloat16)
        result = lax.dot_general(
            weights, value, (((2,), (1,)), ((0,), (0,))), preferred_element_type=jnp.float32
        )
        factor = 1.0 / result[:, :, spare : spare + 1]
        part = (result * factor * mine).reshape(groups * rows, WINDOW)
        columns = pl.ds(start, WINDOW)
        total_ref[:, columns] = total_ref[:, columns] + part


def prepare_kernel(x_ref, mods_ref, first_ref, second_ref, by_x_ref, by_z_ref):
    normed = normalize(x_ref[...].astype(jnp.float32), mods_ref[0:1, :], mods_ref[1:2, :])
    for out_ref, matrix_ref, by_x in ((first_ref, by_x_ref, True), (second_ref, by_z_ref, False)):
        matrix_ref[...] = order_matrix(by_x)
        out_ref[...] = spread_columns(normed, matrix_ref[...])


def spatial_kernel(first_ref, second_ref, x_ref, mods_ref, *refs):
    blocks, order_ref, (out_ref, kept_first, kept_second) = refs[:18], refs[18], refs[19:22]
    w_first, w_second, later_first, later_second, matrix_ref, qkv_ref, total_ref, sems = refs[22:]
    x, zl, c = (lax.axis_index(name) for name in SEQ)
    copies = []

    def bring(target, source, index, low=0, count=PAIR, first=0):
        rows = pl.ds(pl.multiple_of(index * BLOCK, BLOCK), BLOCK)
        target = target.at[rows, low : low + count]
        source = source.at[:, first : first + count]
        copies.append(pltpu.make_async_copy(source, target, sems.at[len(copies)]))
        copies[-1].start()

    for side in range(2):
        own, up, down, far_up, far_down = blocks[9 * side : 9 * side + 5]
        core = c ^ side
        bring(w_first, own, zl * 2 + core)
        bring(w_first, up, ((zl + 3) & 3) * 2 + core)
        bring(w_first, down, ((zl + 1) & 3) * 2 + core)
        bring(w_first, far_up, ((zl + 2) & 3) * 2 + core, 0, CUT)
        bring(w_first, far_down, ((zl + 2) & 3) * 2 + core, CUT, PAIR - CUT)
    for side in range(2):
        core = c ^ side
        for block, apart in zip(blocks[9 * side + 5 : 9 * side + 9], (0, 3, 1, 2)):
            bring(w_second, block, ((x + apart) & 3) * 2 + core)
    for side in range(2):
        core = c ^ side
        own, up, down, _, far_down = blocks[9 * side : 9 * side + 5]
        for block, apart, first in zip((own, up, down, far_down), (0, 3, 1, 2), (PAIR,) * 3 + (PAIR - CUT,)):
            bring(later_first, block, ((zl + apart) & 3) * 2 + core, 0, LEFT, first)
        for block, apart in zip(blocks[9 * side + 5 : 9 * side + 9], (0, 3, 1, 2)):
            bring(later_second, block, ((x + apart) & 3) * 2 + core, 0, RIGHT, PAIR)
    order = pltpu.make_async_copy(order_ref, matrix_ref, sems.at[36])
    order.start()
    total_ref[...] = jnp.zeros_like(total_ref)
    for copy in copies[:10]:
        copy.wait()
    for low in range(0, PAIR, 384):
        part = jnp.dot(first_ref[...], w_first[:, low : low + 384], preferred_element_type=jnp.float32)
        qkv_ref[:, low : low + 384] = part.astype(jnp.bfloat16)
    for copy in copies[10:18]:
        copy.wait()
    for low in range(0, WIDTH, 384):
        part = jnp.dot(second_ref[...], w_second[:, low : low + 384], preferred_element_type=jnp.float32)
        qkv_ref[:, PAIR + low : PAIR + low + 384] = part.astype(jnp.bfloat16)
    for copy in copies[18:]:
        copy.wait()
    keep = [
        pltpu.make_async_copy(later_first, kept_first, sems.at[34]),
        pltpu.make_async_copy(later_second, kept_second, sems.at[35]),
    ]
    for copy in keep:
        copy.start()
    attend(qkv_ref, total_ref, 1, None)
    order.wait()
    attended = spread_columns(total_ref[...].astype(jnp.bfloat16), matrix_ref[...])
    projected = jnp.dot(attended, w_second[:, WIDTH:], preferred_element_type=jnp.float32)
    state = x_ref[...].astype(jnp.float32) + mods_ref[2:3, :] * projected
    out_ref[0:PATCHES, :] = state.astype(jnp.bfloat16)
    out_ref[PATCHES:, :] = jnp.zeros((ROWS - PATCHES, WIDTH), jnp.bfloat16)
    for copy in keep:
        copy.wait()


def temporal_kernel(x_ref, mods_ref, *refs):
    kept_first, kept_second, parts, others, orders = refs[0], refs[1], refs[2:5], refs[5:8], refs[8:10]
    out_ref, w_first, w_second, order_ref, first_ref, second_ref, qkv_ref, total_ref, sems = refs[10:]
    half = ROWS // 2
    x, zl, c = (lax.axis_index(name) for name in SEQ)
    turn = lax.axis_index("y")
    copies = []

    def bring(source, target):
        copies.append(pltpu.make_async_copy(source, target, sems.at[len(copies)]))
        copies[-1].start()

    def rows(index):
        return pl.ds(pl.multiple_of(index * BLOCK, BLOCK), BLOCK)

    for index in range(2):
        bring(orders[index], order_ref.at[index])
    pieces = []
    for side in range(2):
        for part, back in zip((parts, others)[side], (3, 1, 2)):
            for index, apart in enumerate((0, 3, 1, 2)):
                piece = part.at[index * BLOCK : (index + 1) * BLOCK]
                pieces.append((piece, (turn + back) & 3, c ^ side, apart))
    bring(kept_first, w_first.at[turn])
    for piece, owner, core, apart in pieces:
        bring(piece.at[:, :LEFT], w_first.at[owner, rows(((zl + apart) & 3) * 2 + core)])
    bring(kept_second, w_second.at[turn])
    for piece, owner, core, apart in pieces:
        bring(piece.at[:, LEFT:], w_second.at[owner, rows(((x + apart) & 3) * 2 + core)])
    total_ref[...] = jnp.zeros_like(total_ref)
    row = lax.broadcasted_iota(jnp.int32, (half, half), 0)
    column = lax.broadcasted_iota(jnp.int32, (half, half), 1)
    to_patches = jnp.where(column == (row & 31) * 8 + (row >> 5), 1.0, 0.0).astype(jnp.bfloat16)
    to_frames = jnp.where(column == (row & 7) * 32 + (row >> 3), 1.0, 0.0).astype(jnp.bfloat16)
    normed = []
    for sample in range(2):
        state = x_ref[sample * half : (sample + 1) * half, :].astype(jnp.float32)
        state = normalize(state, mods_ref[sample, 0:1, :], mods_ref[sample, 1:2, :])
        normed.append(spread_columns(to_patches, state))
    normed = jnp.concatenate(normed, axis=0)
    for copy in copies[:2]:
        copy.wait()
    for index, target in enumerate((first_ref, second_ref)):
        target[...] = spread_columns(normed, order_ref[index])
    for copy in copies[2:27]:
        copy.wait()
    for index in range(4):
        part = jnp.dot(first_ref[...], w_first[index], preferred_element_type=jnp.float32)
        qkv_ref[:, index * LEFT : (index + 1) * LEFT] = part.astype(jnp.bfloat16)
    for copy in copies[27:]:
        copy.wait()
    for index, count in enumerate((RIGHT, 3 * WIDTH - START - RIGHT)):
        low = START + index * RIGHT
        part = jnp.dot(second_ref[...], w_second[index, :, :count], preferred_element_type=jnp.float32)
        qkv_ref[:, low : low + count] = part.astype(jnp.bfloat16)
    row = lax.broadcasted_iota(jnp.int32, (1, 128, 128), 1)
    column = lax.broadcasted_iota(jnp.int32, (1, 128, 128), 2)
    attend(qkv_ref, total_ref, 4, (row >> 5) == (column >> 5))
    attended = total_ref[...].astype(jnp.bfloat16)
    attended = [
        spread_columns(to_frames, attended[sample * half : (sample + 1) * half]) for sample in range(2)
    ]
    attended = jnp.concatenate(attended, axis=0)
    attended = spread_columns(attended, order_ref[1])
    outward = (w_second[1, :, 3 * WIDTH - START - RIGHT :], w_second[2], w_second[3])
    projected = [jnp.dot(attended, part, preferred_element_type=jnp.float32) for part in outward]
    projected = jnp.concatenate(projected, axis=1)
    results = []
    for sample in range(2):
        state = x_ref[sample * half : (sample + 1) * half, :].astype(jnp.float32)
        state = state + mods_ref[sample, 2:3, :] * projected[sample * half : (sample + 1) * half]
        results.append(state.astype(jnp.bfloat16).astype(jnp.float32))
    cond, uncond = results
    guided = (uncond + 3.0 * (cond - uncond)).reshape(32, 8, WIDTH)
    for sample in range(2):
        both = jnp.concatenate([results[sample].reshape(32, 8, WIDTH), guided], axis=1)
        out_ref[sample * 32 : (sample + 1) * 32] = both.astype(jnp.bfloat16)


def kernel_call(body, out_shape, scratch, flops, moved, specs=None, limit=36, out_specs=None):
    return pl.pallas_call(
        body,
        **({} if specs is None else {"in_specs": specs}),
        **({} if out_specs is None else {"out_specs": out_specs}),
        out_shape=jax.tree.map(
            lambda shape: jax.ShapeDtypeStruct(shape, jnp.bfloat16),
            out_shape,
            is_leaf=lambda shape: isinstance(shape, tuple),
        ),
        scratch_shapes=scratch,
        cost_estimate=pl.CostEstimate(flops=flops, bytes_accessed=moved, transcendentals=0),
        compiler_params=pltpu.CompilerParams(vmem_limit_bytes=limit * 2**20),
    )


def along(block, axis, by):
    return lax.ppermute(block, axis, [(i, (i + by) % 4) for i in range(4)])


def along_z(block, by):
    def index(z):
        return z % 4 * 2 + z // 4

    return lax.ppermute(block, ("zl", "zh"), [(index(z), index((z + by) % 8)) for z in range(8)])


def other_core(block):
    return lax.ppermute(block, "c", [(0, 1), (1, 0)])


def gather_weights(w_qkv, w_out, state, early_mods, mods):
    turn = lax.axis_index("y")
    later = jnp.concatenate([w_qkv[1], w_out[1]], axis=1)
    later_first = lax.dynamic_slice(later, (0, turn * LEFT), (SHARD, LEFT))
    later_second = lax.dynamic_slice(later, (0, START + turn * RIGHT), (SHARD, RIGHT))
    first = jnp.concatenate([w_qkv[0, :, :PAIR], later_first], axis=1)
    second = jnp.concatenate([w_qkv[0, :, PAIR:], w_out[0], later_second], axis=1)
    up, down, far = along(first, "x", 1), along(first, "x", 3), along(first, "x", 2)
    up_z, down_z = along_z(second, 1), along_z(second, 7)
    far_z = lax.ppermute(second, "zl", [(0, 2), (2, 0), (1, 3), (3, 1)])
    first = jnp.concatenate([first, down, far, up], axis=0)
    second = jnp.concatenate([second, down_z, far_z, up_z], axis=0)
    first, second, state = lax.optimization_barrier((first, second, state))
    shapes = [(PATCHES, WIDTH)] * 2 + [(WIDTH, WIDTH)] * 2
    prepared = kernel_call(prepare_kernel, shapes, [], 10**10, 10**7)(state, early_mods)
    near = [along_z(first, 1), along_z(first, 7), along(second, "x", 1), along(second, "x", 3)]
    own_other = [other_core(first), other_core(second)]
    first_far, second_far, near, mods, prepared = lax.optimization_barrier(
        (first, second, near, mods, prepared)
    )
    far = [along_z(first_far[:, :CUT], 2), along_z(first_far[:, CUT:], 6), along(second_far, "x", 2)]
    near_other = [other_core(block) for block in near]
    mine = [first] + near[:2] + far[:2] + [second] + near[2:] + far[2:]
    left = [block[:, PAIR:] for block in mine[:3]] + [mine[4][:, PAIR - CUT :]]
    right = [block[:, PAIR:] for block in mine[5:]]
    share = jnp.concatenate(
        [jnp.concatenate(left, axis=0), jnp.concatenate(right, axis=0)], axis=1
    )
    other = lax.ppermute(mods, "zh", [(0, 1), (1, 0)])
    leads = lax.axis_index("zh") == 0
    mods = jnp.stack([jnp.where(leads, mods, other), jnp.where(leads, other, mods)])
    share, mods = lax.optimization_barrier((share, mods))
    far_other = [other_core(block) for block in far]
    theirs = own_other[:1] + near_other[:2] + far_other[:2]
    theirs += own_other[1:] + near_other[2:] + far_other[2:]
    parts = [along(share, "y", by) for by in (1, 3, 2)]
    return mine + theirs, parts + [other_core(part) for part in parts], prepared, mods


def on_device(hidden, modulation, w_qkv, w_out):
    state = hidden.reshape(PATCHES, WIDTH)
    mods = modulation[0]

    weights, later, prepared, both_mods = gather_weights(w_qkv, w_out, state, mods[0], mods[1])
    first, second, by_x, by_z = prepared
    layer_one, kept_first, kept_second = kernel_call(
        spatial_kernel,
        [(ROWS, WIDTH), (WIDTH, LEFT), (WIDTH, RIGHT)],
        [
            pltpu.VMEM((WIDTH, PAIR), jnp.bfloat16),
            pltpu.VMEM((WIDTH, PAIR), jnp.bfloat16),
            pltpu.VMEM((WIDTH, LEFT), jnp.bfloat16),
            pltpu.VMEM((WIDTH, RIGHT), jnp.bfloat16),
            pltpu.VMEM((WIDTH, WIDTH), jnp.bfloat16),
            pltpu.VMEM((PATCHES, 3 * WIDTH), jnp.bfloat16),
            pltpu.VMEM((PATCHES, WIDTH), jnp.float32),
            pltpu.SemaphoreType.DMA((37,)),
        ],
        10**10,
        2 * 10**7,
        [pl.BlockSpec(memory_space=pltpu.VMEM)] * 4 + [pl.BlockSpec(memory_space=pl.ANY)] * 19,
        38,
        [pl.BlockSpec(memory_space=pltpu.VMEM)] + [pl.BlockSpec(memory_space=pltpu.HBM)] * 2,
    )(first, second, state, mods[0], *weights, by_z)
    by_patch = lax.all_to_all(layer_one.reshape(64, 8, WIDTH), PAIRED, 0, 0, tiled=True)
    result = kernel_call(
        temporal_kernel,
        (64, 16, WIDTH),
        [
            pltpu.VMEM((4, WIDTH, LEFT), jnp.bfloat16),
            pltpu.VMEM((4, WIDTH, RIGHT), jnp.bfloat16),
            pltpu.VMEM((2, WIDTH, WIDTH), jnp.bfloat16),
            pltpu.VMEM((ROWS, WIDTH), jnp.bfloat16),
            pltpu.VMEM((ROWS, WIDTH), jnp.bfloat16),
            pltpu.VMEM((ROWS, 3 * WIDTH), jnp.bfloat16),
            pltpu.VMEM((ROWS, WIDTH), jnp.float32),
            pltpu.SemaphoreType.DMA((52,)),
        ],
        10**10,
        2 * 10**7,
        [pl.BlockSpec(memory_space=pltpu.VMEM)] * 2 + [pl.BlockSpec(memory_space=pltpu.HBM)] * 10,
        58,
    )(by_patch.reshape(ROWS, WIDTH), both_mods, kept_first, kept_second, *later, by_x, by_z)
    by_frame = lax.all_to_all(result, PAIRED, 0, 0, tiled=True)
    hidden_out = by_frame[:, :8].reshape(ROWS, WIDTH)[:PATCHES]
    guided = by_frame[:, 8:].reshape(ROWS, WIDTH)[:PATCHES]
    return hidden_out.reshape(hidden.shape), guided.reshape(hidden.shape)


def solution(mesh):
    split = Mesh(mesh.devices.reshape(4, 4, 2, 4, 2), ("x", "zl", "c", "y", "zh"))
    batch, seq = ("y", "zh"), SEQ
    placed = (
        P(batch, seq, None, None),
        P(batch, None, None, None),
        P(None, seq, None),
        P(None, seq, None),
    )
    return jax.shard_map(
        on_device,
        mesh=split,
        in_specs=placed,
        out_specs=(P(batch, seq, None, None), P(batch, seq, None, None)),
        check_vma=False,
    )
```

```python
import jax
import jax.numpy as jnp
from jax import lax
from jax.experimental import pallas as pl
from jax.experimental.pallas import tpu as pltpu
from jax.sharding import Mesh, PartitionSpec as P

HEADS = 16
SIZE = 72
WIDTH = HEADS * SIZE
SHARD = 36
WINDOW = 256
PATCHES = 448
ROWS = 512
EXPONENT = SIZE**-0.5 * 1.4426950408889634
SEQ = ("x", "zl", "c")
PAIRED = ("zh", "x", "zl", "c")
BLOCK = 4 * SHARD
PAIR = 2 * WIDTH
LEFT = 640
RIGHT = WIDTH - LEFT
FIRST = PAIR + LEFT
START = 4 * LEFT
CUT = 1536


def normalize(state, shift, scale):
    mean = jnp.mean(state, axis=-1, keepdims=True)
    centered = state - mean
    spread = jnp.mean(centered * centered, axis=-1, keepdims=True)
    return (centered * lax.rsqrt(spread + 1e-06) * (1.0 + scale) + shift).astype(jnp.bfloat16)


def order_matrix(by_x):
    feature = lax.broadcasted_iota(jnp.int32, (WIDTH, 1), 0)
    x, zl, c, row = feature // 288, (feature // 72) & 3, (feature // 36) & 1, feature % SHARD
    if by_x:
        place = (zl * 2 + c) * 4 + ((x - lax.axis_index("x")) & 3)
    else:
        place = (x * 2 + c) * 4 + ((zl - lax.axis_index("zl")) & 3)
    column = lax.broadcasted_iota(jnp.int32, (WIDTH, WIDTH), 1)
    return jnp.where(column == place * SHARD + row, 1.0, 0.0).astype(jnp.bfloat16)


def spread_columns(block, matrix):
    return jnp.dot(block, matrix, preferred_element_type=jnp.float32).astype(jnp.bfloat16)


def attend(qkv_ref, total_ref, groups, allowed):
    rows = qkv_ref.shape[0] // groups
    lane = lax.broadcasted_iota(jnp.int32, (1, 1, WINDOW), 2)
    for head in range(HEADS):
        start = min(head * SIZE // 128 * 128, WIDTH - WINDOW)
        inner = head * SIZE - start
        spare = 0 if inner > 0 else WINDOW - 1
        mine = jnp.where((lane >= inner) & (lane < inner + SIZE), 1.0, 0.0)
        mask = mine.astype(jnp.bfloat16)
        unit = jnp.where(lane == spare, 1.0, 0.0).astype(jnp.bfloat16)

        def window(first):
            return qkv_ref[:, first + start : first + start + WINDOW].reshape(groups, rows, WINDOW)

        query, key, value = window(0) * mask, window(WIDTH), window(2 * WIDTH) * mask + unit
        scores = lax.dot_general(
            query, key, (((2,), (2,)), ((0,), (0,))), preferred_element_type=jnp.float32
        )
        if allowed is not None:
            scores = jnp.where(allowed, scores, -jnp.inf)
        top = jnp.max(scores, axis=2, keepdims=True)
        weights = jnp.exp2((scores - top) * EXPONENT).astype(jnp.bfloat16)
        result = lax.dot_general(
            weights, value, (((2,), (1,)), ((0,), (0,))), preferred_element_type=jnp.float32
        )
        factor = 1.0 / result[:, :, spare : spare + 1]
        part = (result * factor * mine).reshape(groups * rows, WINDOW)
        columns = pl.ds(start, WINDOW)
        total_ref[:, columns] = total_ref[:, columns] + part


def prepare_kernel(x_ref, mods_ref, first_ref, second_ref, by_x_ref, by_z_ref, order_ref, sems):
    copies = []
    for index, (out_ref, by_x) in enumerate(((by_x_ref, True), (by_z_ref, False))):
        order_ref[index] = order_matrix(by_x)
        copies.append(pltpu.make_async_copy(order_ref.at[index], out_ref, sems.at[index]))
        copies[-1].start()
    normed = normalize(x_ref[...].astype(jnp.float32), mods_ref[0:1, :], mods_ref[1:2, :])
    for index, out_ref in enumerate((first_ref, second_ref)):
        out_ref[...] = spread_columns(normed, order_ref[index])
    for copy in copies:
        copy.wait()


def spatial_kernel(first_ref, second_ref, x_ref, mods_ref, *refs):
    blocks, order_ref, (out_ref, kept_first, kept_second) = refs[:18], refs[18], refs[19:22]
    w_first, w_second, later_first, later_second, matrix_ref, qkv_ref, total_ref, sems = refs[22:]
    x, zl, c = (lax.axis_index(name) for name in SEQ)
    copies = []

    def bring(target, source, index, low=0, count=PAIR, first=0):
        rows = pl.ds(pl.multiple_of(index * BLOCK, BLOCK), BLOCK)
        target = target.at[rows, low : low + count]
        source = source.at[:, first : first + count]
        copies.append(pltpu.make_async_copy(source, target, sems.at[len(copies)]))
        copies[-1].start()

    for side in range(2):
        own, up, down, far_up, far_down = blocks[9 * side : 9 * side + 5]
        core = c ^ side
        bring(w_first, own, zl * 2 + core)
        bring(w_first, up, ((zl + 3) & 3) * 2 + core)
        bring(w_first, down, ((zl + 1) & 3) * 2 + core)
        bring(w_first, far_up, ((zl + 2) & 3) * 2 + core, 0, CUT)
        bring(w_first, far_down, ((zl + 2) & 3) * 2 + core, CUT, PAIR - CUT)
    for side in range(2):
        core = c ^ side
        for block, apart in zip(blocks[9 * side + 5 : 9 * side + 9], (0, 3, 1, 2)):
            bring(w_second, block, ((x + apart) & 3) * 2 + core)
    for side in range(2):
        core = c ^ side
        own, up, down, _, far_down = blocks[9 * side : 9 * side + 5]
        for block, apart, first in zip((own, up, down, far_down), (0, 3, 1, 2), (PAIR,) * 3 + (PAIR - CUT,)):
            bring(later_first, block, ((zl + apart) & 3) * 2 + core, 0, LEFT, first)
        for block, apart in zip(blocks[9 * side + 5 : 9 * side + 9], (0, 3, 1, 2)):
            bring(later_second, block, ((x + apart) & 3) * 2 + core, 0, RIGHT, PAIR)
    order = pltpu.make_async_copy(order_ref, matrix_ref, sems.at[36])
    order.start()
    total_ref[...] = jnp.zeros_like(total_ref)
    for copy in copies[:10]:
        copy.wait()
    for low in range(0, PAIR, 384):
        part = jnp.dot(first_ref[...], w_first[:, low : low + 384], preferred_element_type=jnp.float32)
        qkv_ref[:, low : low + 384] = part.astype(jnp.bfloat16)
    for copy in copies[10:18]:
        copy.wait()
    for low in range(0, WIDTH, 384):
        part = jnp.dot(second_ref[...], w_second[:, low : low + 384], preferred_element_type=jnp.float32)
        qkv_ref[:, PAIR + low : PAIR + low + 384] = part.astype(jnp.bfloat16)
    for copy in copies[18:]:
        copy.wait()
    keep = [
        pltpu.make_async_copy(later_first, kept_first, sems.at[34]),
        pltpu.make_async_copy(later_second, kept_second, sems.at[35]),
    ]
    for copy in keep:
        copy.start()
    attend(qkv_ref, total_ref, 1, None)
    order.wait()
    attended = spread_columns(total_ref[...].astype(jnp.bfloat16), matrix_ref[...])
    projected = jnp.dot(attended, w_second[:, WIDTH:], preferred_element_type=jnp.float32)
    state = x_ref[...].astype(jnp.float32) + mods_ref[2:3, :] * projected
    out_ref[0:PATCHES, :] = state.astype(jnp.bfloat16)
    out_ref[PATCHES:, :] = jnp.zeros((ROWS - PATCHES, WIDTH), jnp.bfloat16)
    for copy in keep:
        copy.wait()


def temporal_kernel(x_ref, mods_ref, *refs):
    kept_first, kept_second, parts, others, orders = refs[0], refs[1], refs[2:5], refs[5:8], refs[8:10]
    out_ref, w_first, w_second, order_ref, first_ref, second_ref, qkv_ref, total_ref, sems = refs[10:]
    half = ROWS // 2
    x, zl, c = (lax.axis_index(name) for name in SEQ)
    turn = lax.axis_index("y")
    copies = []

    def bring(source, target):
        copies.append(pltpu.make_async_copy(source, target, sems.at[len(copies)]))
        copies[-1].start()

    def rows(index):
        return pl.ds(pl.multiple_of(index * BLOCK, BLOCK), BLOCK)

    for index in range(2):
        bring(orders[index], order_ref.at[index])
    pieces = []
    for side in range(2):
        for part, back in zip((parts, others)[side], (3, 1, 2)):
            for index, apart in enumerate((0, 3, 1, 2)):
                piece = part.at[index * BLOCK : (index + 1) * BLOCK]
                pieces.append((piece, (turn + back) & 3, c ^ side, apart))
    bring(kept_first, w_first.at[turn])
    for piece, owner, core, apart in pieces:
        bring(piece.at[:, :LEFT], w_first.at[owner, rows(((zl + apart) & 3) * 2 + core)])
    bring(kept_second, w_second.at[turn])
    for piece, owner, core, apart in pieces:
        bring(piece.at[:, LEFT:], w_second.at[owner, rows(((x + apart) & 3) * 2 + core)])
    total_ref[...] = jnp.zeros_like(total_ref)
    row = lax.broadcasted_iota(jnp.int32, (half, half), 0)
    column = lax.broadcasted_iota(jnp.int32, (half, half), 1)
    to_patches = jnp.where(column == (row & 31) * 8 + (row >> 5), 1.0, 0.0).astype(jnp.bfloat16)
    to_frames = jnp.where(column == (row & 7) * 32 + (row >> 3), 1.0, 0.0).astype(jnp.bfloat16)
    normed = []
    for sample in range(2):
        state = x_ref[sample * half : (sample + 1) * half, :].astype(jnp.float32)
        state = normalize(state, mods_ref[sample, 0:1, :], mods_ref[sample, 1:2, :])
        normed.append(spread_columns(to_patches, state))
    normed = jnp.concatenate(normed, axis=0)
    for copy in copies[:2]:
        copy.wait()
    for index, target in enumerate((first_ref, second_ref)):
        target[...] = spread_columns(normed, order_ref[index])
    for copy in copies[2:27]:
        copy.wait()
    for index in range(4):
        part = jnp.dot(first_ref[...], w_first[index], preferred_element_type=jnp.float32)
        qkv_ref[:, index * LEFT : (index + 1) * LEFT] = part.astype(jnp.bfloat16)
    for copy in copies[27:]:
        copy.wait()
    for index, count in enumerate((RIGHT, 3 * WIDTH - START - RIGHT)):
        low = START + index * RIGHT
        part = jnp.dot(second_ref[...], w_second[index, :, :count], preferred_element_type=jnp.float32)
        qkv_ref[:, low : low + count] = part.astype(jnp.bfloat16)
    row = lax.broadcasted_iota(jnp.int32, (1, 128, 128), 1)
    column = lax.broadcasted_iota(jnp.int32, (1, 128, 128), 2)
    attend(qkv_ref, total_ref, 4, (row >> 5) == (column >> 5))
    attended = total_ref[...].astype(jnp.bfloat16)
    attended = [
        spread_columns(to_frames, attended[sample * half : (sample + 1) * half]) for sample in range(2)
    ]
    attended = jnp.concatenate(attended, axis=0)
    attended = spread_columns(attended, order_ref[1])
    outward = (w_second[1, :, 3 * WIDTH - START - RIGHT :], w_second[2], w_second[3])
    projected = [jnp.dot(attended, part, preferred_element_type=jnp.float32) for part in outward]
    projected = jnp.concatenate(projected, axis=1)
    results = []
    for sample in range(2):
        state = x_ref[sample * half : (sample + 1) * half, :].astype(jnp.float32)
        state = state + mods_ref[sample, 2:3, :] * projected[sample * half : (sample + 1) * half]
        results.append(state.astype(jnp.bfloat16).astype(jnp.float32))
    cond, uncond = results
    guided = (uncond + 3.0 * (cond - uncond)).reshape(32, 8, WIDTH)
    for sample in range(2):
        both = jnp.concatenate([results[sample].reshape(32, 8, WIDTH), guided], axis=1)
        out_ref[sample * 32 : (sample + 1) * 32] = both.astype(jnp.bfloat16)


def kernel_call(body, out_shape, scratch, flops, moved, specs=None, limit=36, out_specs=None):
    return pl.pallas_call(
        body,
        **({} if specs is None else {"in_specs": specs}),
        **({} if out_specs is None else {"out_specs": out_specs}),
        out_shape=jax.tree.map(
            lambda shape: jax.ShapeDtypeStruct(shape, jnp.bfloat16),
            out_shape,
            is_leaf=lambda shape: isinstance(shape, tuple),
        ),
        scratch_shapes=scratch,
        cost_estimate=pl.CostEstimate(flops=flops, bytes_accessed=moved, transcendentals=0),
        compiler_params=pltpu.CompilerParams(vmem_limit_bytes=limit * 2**20),
    )


def along(block, axis, by):
    return lax.ppermute(block, axis, [(i, (i + by) % 4) for i in range(4)])


def along_z(block, by):
    def index(z):
        return z % 4 * 2 + z // 4

    return lax.ppermute(block, ("zl", "zh"), [(index(z), index((z + by) % 8)) for z in range(8)])


def other_core(block):
    return lax.ppermute(block, "c", [(0, 1), (1, 0)])


def gather_weights(w_qkv, w_out, state, mods):
    turn = lax.axis_index("y")
    later = jnp.concatenate([w_qkv[1], w_out[1]], axis=1)
    later_first = lax.dynamic_slice(later, (0, turn * LEFT), (SHARD, LEFT))
    later_second = lax.dynamic_slice(later, (0, START + turn * RIGHT), (SHARD, RIGHT))
    first = jnp.concatenate([w_qkv[0, :, :PAIR], later_first], axis=1)
    second = jnp.concatenate([w_qkv[0, :, PAIR:], w_out[0], later_second], axis=1)
    up, down, far = along(first, "x", 1), along(first, "x", 3), along(first, "x", 2)
    up_z, down_z = along_z(second, 1), along_z(second, 7)
    far_z = lax.ppermute(second, "zl", [(0, 2), (2, 0), (1, 3), (3, 1)])
    first = jnp.concatenate([first, down, far, up], axis=0)
    second = jnp.concatenate([second, down_z, far_z, up_z], axis=0)
    first, second, state = lax.optimization_barrier((first, second, state))
    near = [along_z(first, 1), along_z(first, 7), along(second, "x", 1), along(second, "x", 3)]
    own_other = [other_core(first), other_core(second)]
    first_far, second_far, near, mods = lax.optimization_barrier((first, second, near, mods))
    far = [along_z(first_far[:, :CUT], 2), along_z(first_far[:, CUT:], 6), along(second_far, "x", 2)]
    near_other = [other_core(block) for block in near]
    mine = [first] + near[:2] + far[:2] + [second] + near[2:] + far[2:]
    left = [block[:, PAIR:] for block in mine[:3]] + [mine[4][:, PAIR - CUT :]]
    right = [block[:, PAIR:] for block in mine[5:]]
    share = jnp.concatenate(
        [jnp.concatenate(left, axis=0), jnp.concatenate(right, axis=0)], axis=1
    )
    other = lax.ppermute(mods, "zh", [(0, 1), (1, 0)])
    leads = lax.axis_index("zh") == 0
    mods = jnp.stack([jnp.where(leads, mods, other), jnp.where(leads, other, mods)])
    share, mods = lax.optimization_barrier((share, mods))
    far_other = [other_core(block) for block in far]
    theirs = own_other[:1] + near_other[:2] + far_other[:2]
    theirs += own_other[1:] + near_other[2:] + far_other[2:]
    parts = [along(share, "y", by) for by in (1, 3, 2)]
    return mine + theirs, parts + [other_core(part) for part in parts], state, mods


def on_device(hidden, modulation, w_qkv, w_out):
    state = hidden.reshape(PATCHES, WIDTH)
    mods = modulation[0]

    weights, later, late_state, both_mods = gather_weights(w_qkv, w_out, state, mods[1])
    first, second, by_x, by_z = kernel_call(
        prepare_kernel,
        [(PATCHES, WIDTH)] * 2 + [(WIDTH, WIDTH)] * 2,
        [pltpu.VMEM((2, WIDTH, WIDTH), jnp.bfloat16), pltpu.SemaphoreType.DMA((2,))],
        10**10,
        10**7,
        [pl.BlockSpec(memory_space=pltpu.VMEM)] * 2,
        36,
        [pl.BlockSpec(memory_space=pltpu.VMEM)] * 2 + [pl.BlockSpec(memory_space=pltpu.HBM)] * 2,
    )(late_state, mods[0])
    layer_one, kept_first, kept_second = kernel_call(
        spatial_kernel,
        [(ROWS, WIDTH), (WIDTH, LEFT), (WIDTH, RIGHT)],
        [
            pltpu.VMEM((WIDTH, PAIR), jnp.bfloat16),
            pltpu.VMEM((WIDTH, PAIR), jnp.bfloat16),
            pltpu.VMEM((WIDTH, LEFT), jnp.bfloat16),
            pltpu.VMEM((WIDTH, RIGHT), jnp.bfloat16),
            pltpu.VMEM((WIDTH, WIDTH), jnp.bfloat16),
            pltpu.VMEM((PATCHES, 3 * WIDTH), jnp.bfloat16),
            pltpu.VMEM((PATCHES, WIDTH), jnp.float32),
            pltpu.SemaphoreType.DMA((37,)),
        ],
        10**10,
        2 * 10**7,
        [pl.BlockSpec(memory_space=pltpu.VMEM)] * 4 + [pl.BlockSpec(memory_space=pl.ANY)] * 19,
        38,
        [pl.BlockSpec(memory_space=pltpu.VMEM)] + [pl.BlockSpec(memory_space=pltpu.HBM)] * 2,
    )(first, second, state, mods[0], *weights, by_z)
    by_patch = lax.all_to_all(layer_one.reshape(64, 8, WIDTH), PAIRED, 0, 0, tiled=True)
    result = kernel_call(
        temporal_kernel,
        (64, 16, WIDTH),
        [
            pltpu.VMEM((4, WIDTH, LEFT), jnp.bfloat16),
            pltpu.VMEM((4, WIDTH, RIGHT), jnp.bfloat16),
            pltpu.VMEM((2, WIDTH, WIDTH), jnp.bfloat16),
            pltpu.VMEM((ROWS, WIDTH), jnp.bfloat16),
            pltpu.VMEM((ROWS, WIDTH), jnp.bfloat16),
            pltpu.VMEM((ROWS, 3 * WIDTH), jnp.bfloat16),
            pltpu.VMEM((ROWS, WIDTH), jnp.float32),
            pltpu.SemaphoreType.DMA((52,)),
        ],
        10**10,
        2 * 10**7,
        [pl.BlockSpec(memory_space=pltpu.VMEM)] * 2 + [pl.BlockSpec(memory_space=pltpu.HBM)] * 10,
        58,
    )(by_patch.reshape(ROWS, WIDTH), both_mods, kept_first, kept_second, *later, by_x, by_z)
    by_frame = lax.all_to_all(result, PAIRED, 0, 0, tiled=True)
    hidden_out = by_frame[:, :8].reshape(ROWS, WIDTH)[:PATCHES]
    guided = by_frame[:, 8:].reshape(ROWS, WIDTH)[:PATCHES]
    return hidden_out.reshape(hidden.shape), guided.reshape(hidden.shape)


def solution(mesh):
    split = Mesh(mesh.devices.reshape(4, 4, 2, 4, 2), ("x", "zl", "c", "y", "zh"))
    batch, seq = ("y", "zh"), SEQ
    placed = (
        P(batch, seq, None, None),
        P(batch, None, None, None),
        P(None, seq, None),
        P(None, seq, None),
    )
    return jax.shard_map(
        on_device,
        mesh=split,
        in_specs=placed,
        out_specs=(P(batch, seq, None, None), P(batch, seq, None, None)),
        check_vma=False,
    )
```

```python
import jax
import jax.numpy as jnp
from jax import lax
from jax.experimental import pallas as pl
from jax.experimental.pallas import tpu as pltpu
from jax.sharding import Mesh, PartitionSpec as P

HEADS = 16
SIZE = 72
WIDTH = HEADS * SIZE
SHARD = 36
WINDOW = 256
PATCHES = 448
ROWS = 512
EXPONENT = SIZE**-0.5 * 1.4426950408889634
SEQ = ("x", "zl", "c")
PAIRED = ("zh", "x", "zl", "c")
BLOCK = 4 * SHARD
PAIR = 2 * WIDTH
LEFT = 640
RIGHT = WIDTH - LEFT
FIRST = PAIR + LEFT
START = 4 * LEFT
CUT = 1536


def normalize(state, shift, scale):
    mean = jnp.mean(state, axis=-1, keepdims=True)
    centered = state - mean
    spread = jnp.mean(centered * centered, axis=-1, keepdims=True)
    return (centered * lax.rsqrt(spread + 1e-06) * (1.0 + scale) + shift).astype(jnp.bfloat16)


def order_matrix(by_x):
    feature = lax.broadcasted_iota(jnp.int32, (WIDTH, 1), 0)
    x, zl, c, row = feature // 288, (feature // 72) & 3, (feature // 36) & 1, feature % SHARD
    if by_x:
        place = (zl * 2 + c) * 4 + ((x - lax.axis_index("x")) & 3)
    else:
        place = (x * 2 + c) * 4 + ((zl - lax.axis_index("zl")) & 3)
    column = lax.broadcasted_iota(jnp.int32, (WIDTH, WIDTH), 1)
    return jnp.where(column == place * SHARD + row, 1.0, 0.0).astype(jnp.bfloat16)


def spread_columns(block, matrix):
    return jnp.dot(block, matrix, preferred_element_type=jnp.float32).astype(jnp.bfloat16)


def attend(qkv_ref, total_ref, groups, allowed):
    rows = qkv_ref.shape[0] // groups
    lane = lax.broadcasted_iota(jnp.int32, (1, 1, WINDOW), 2)
    for head in range(HEADS):
        start = min(head * SIZE // 128 * 128, WIDTH - WINDOW)
        inner = head * SIZE - start
        spare = 0 if inner > 0 else WINDOW - 1
        mine = jnp.where((lane >= inner) & (lane < inner + SIZE), 1.0, 0.0)
        mask = mine.astype(jnp.bfloat16)
        unit = jnp.where(lane == spare, 1.0, 0.0).astype(jnp.bfloat16)

        def window(first):
            return qkv_ref[:, first + start : first + start + WINDOW].reshape(groups, rows, WINDOW)

        query, key, value = window(0) * mask, window(WIDTH), window(2 * WIDTH) * mask + unit
        scores = lax.dot_general(
            query, key, (((2,), (2,)), ((0,), (0,))), preferred_element_type=jnp.float32
        )
        if allowed is not None:
            scores = jnp.where(allowed, scores, -jnp.inf)
        top = jnp.max(scores, axis=2, keepdims=True)
        weights = jnp.exp2((scores - top) * EXPONENT).astype(jnp.bfloat16)
        result = lax.dot_general(
            weights, value, (((2,), (1,)), ((0,), (0,))), preferred_element_type=jnp.float32
        )
        factor = 1.0 / result[:, :, spare : spare + 1]
        part = (result * factor * mine).reshape(groups * rows, WINDOW)
        columns = pl.ds(start, WINDOW)
        total_ref[:, columns] = total_ref[:, columns] + part


def prepare_kernel(x_ref, mods_ref, first_ref, second_ref):
    normed = normalize(x_ref[...].astype(jnp.float32), mods_ref[0:1, :], mods_ref[1:2, :])
    first_ref[...] = spread_columns(normed, order_matrix(True))
    second_ref[...] = spread_columns(normed, order_matrix(False))


def order_kernel(_, by_x_ref, by_z_ref):
    by_x_ref[...] = order_matrix(True)
    by_z_ref[...] = order_matrix(False)


def spatial_kernel(first_ref, second_ref, x_ref, mods_ref, *refs):
    blocks, (out_ref, kept_first, kept_second) = refs[:18], refs[18:21]
    w_first, w_second, later_first, later_second, matrix_ref, qkv_ref, total_ref, sems = refs[21:]
    x, zl, c = (lax.axis_index(name) for name in SEQ)
    copies = []

    def bring(target, source, index, low=0, count=PAIR, first=0):
        rows = pl.ds(pl.multiple_of(index * BLOCK, BLOCK), BLOCK)
        target = target.at[rows, low : low + count]
        source = source.at[:, first : first + count]
        copies.append(pltpu.make_async_copy(source, target, sems.at[len(copies)]))
        copies[-1].start()

    for side in range(2):
        own, up, down, far_up, far_down = blocks[9 * side : 9 * side + 5]
        core = c ^ side
        bring(w_first, own, zl * 2 + core)
        bring(w_first, up, ((zl + 3) & 3) * 2 + core)
        bring(w_first, down, ((zl + 1) & 3) * 2 + core)
        bring(w_first, far_up, ((zl + 2) & 3) * 2 + core, 0, CUT)
        bring(w_first, far_down, ((zl + 2) & 3) * 2 + core, CUT, PAIR - CUT)
    for side in range(2):
        core = c ^ side
        for block, apart in zip(blocks[9 * side + 5 : 9 * side + 9], (0, 3, 1, 2)):
            bring(w_second, block, ((x + apart) & 3) * 2 + core)
    for side in range(2):
        core = c ^ side
        own, up, down, _, far_down = blocks[9 * side : 9 * side + 5]
        for block, apart, first in zip((own, up, down, far_down), (0, 3, 1, 2), (PAIR,) * 3 + (PAIR - CUT,)):
            bring(later_first, block, ((zl + apart) & 3) * 2 + core, 0, LEFT, first)
        for block, apart in zip(blocks[9 * side + 5 : 9 * side + 9], (0, 3, 1, 2)):
            bring(later_second, block, ((x + apart) & 3) * 2 + core, 0, RIGHT, PAIR)
    matrix_ref[...] = order_matrix(False)
    total_ref[...] = jnp.zeros_like(total_ref)
    for copy in copies[:10]:
        copy.wait()
    for low in range(0, PAIR, 384):
        part = jnp.dot(first_ref[...], w_first[:, low : low + 384], preferred_element_type=jnp.float32)
        qkv_ref[:, low : low + 384] = part.astype(jnp.bfloat16)
    for copy in copies[10:18]:
        copy.wait()
    for low in range(0, WIDTH, 384):
        part = jnp.dot(second_ref[...], w_second[:, low : low + 384], preferred_element_type=jnp.float32)
        qkv_ref[:, PAIR + low : PAIR + low + 384] = part.astype(jnp.bfloat16)
    for copy in copies[18:]:
        copy.wait()
    keep = [
        pltpu.make_async_copy(later_first, kept_first, sems.at[34]),
        pltpu.make_async_copy(later_second, kept_second, sems.at[35]),
    ]
    for copy in keep:
        copy.start()
    attend(qkv_ref, total_ref, 1, None)
    attended = spread_columns(total_ref[...].astype(jnp.bfloat16), matrix_ref[...])
    projected = jnp.dot(attended, w_second[:, WIDTH:], preferred_element_type=jnp.float32)
    state = x_ref[...].astype(jnp.float32) + mods_ref[2:3, :] * projected
    out_ref[0:PATCHES, :] = state.astype(jnp.bfloat16)
    out_ref[PATCHES:, :] = jnp.zeros((ROWS - PATCHES, WIDTH), jnp.bfloat16)
    for copy in keep:
        copy.wait()


def temporal_kernel(x_ref, mods_ref, *refs):
    kept_first, kept_second, parts, others, orders = refs[0], refs[1], refs[2:5], refs[5:8], refs[8:10]
    out_ref, w_first, w_second, order_ref, first_ref, second_ref, qkv_ref, total_ref, sems = refs[10:]
    half = ROWS // 2
    x, zl, c = (lax.axis_index(name) for name in SEQ)
    turn = lax.axis_index("y")
    copies = []

    def bring(source, target):
        copies.append(pltpu.make_async_copy(source, target, sems.at[len(copies)]))
        copies[-1].start()

    def rows(index):
        return pl.ds(pl.multiple_of(index * BLOCK, BLOCK), BLOCK)

    for index in range(2):
        bring(orders[index], order_ref.at[index])
    pieces = []
    for side in range(2):
        for part, back in zip((parts, others)[side], (3, 1, 2)):
            for index, apart in enumerate((0, 3, 1, 2)):
                piece = part.at[index * BLOCK : (index + 1) * BLOCK]
                pieces.append((piece, (turn + back) & 3, c ^ side, apart))
    bring(kept_first, w_first.at[turn])
    for piece, owner, core, apart in pieces:
        bring(piece.at[:, :LEFT], w_first.at[owner, rows(((zl + apart) & 3) * 2 + core)])
    bring(kept_second, w_second.at[turn])
    for piece, owner, core, apart in pieces:
        bring(piece.at[:, LEFT:], w_second.at[owner, rows(((x + apart) & 3) * 2 + core)])
    total_ref[...] = jnp.zeros_like(total_ref)
    row = lax.broadcasted_iota(jnp.int32, (half, half), 0)
    column = lax.broadcasted_iota(jnp.int32, (half, half), 1)
    to_patches = jnp.where(column == (row & 31) * 8 + (row >> 5), 1.0, 0.0).astype(jnp.bfloat16)
    to_frames = jnp.where(column == (row & 7) * 32 + (row >> 3), 1.0, 0.0).astype(jnp.bfloat16)
    normed = []
    for sample in range(2):
        state = x_ref[sample * half : (sample + 1) * half, :].astype(jnp.float32)
        state = normalize(state, mods_ref[sample, 0:1, :], mods_ref[sample, 1:2, :])
        normed.append(spread_columns(to_patches, state))
    normed = jnp.concatenate(normed, axis=0)
    for copy in copies[:2]:
        copy.wait()
    for index, target in enumerate((first_ref, second_ref)):
        target[...] = spread_columns(normed, order_ref[index])
    for copy in copies[2:27]:
        copy.wait()
    for index in range(4):
        part = jnp.dot(first_ref[...], w_first[index], preferred_element_type=jnp.float32)
        qkv_ref[:, index * LEFT : (index + 1) * LEFT] = part.astype(jnp.bfloat16)
    for copy in copies[27:]:
        copy.wait()
    for index, count in enumerate((RIGHT, 3 * WIDTH - START - RIGHT)):
        low = START + index * RIGHT
        part = jnp.dot(second_ref[...], w_second[index, :, :count], preferred_element_type=jnp.float32)
        qkv_ref[:, low : low + count] = part.astype(jnp.bfloat16)
    row = lax.broadcasted_iota(jnp.int32, (1, 128, 128), 1)
    column = lax.broadcasted_iota(jnp.int32, (1, 128, 128), 2)
    attend(qkv_ref, total_ref, 4, (row >> 5) == (column >> 5))
    attended = total_ref[...].astype(jnp.bfloat16)
    attended = [
        spread_columns(to_frames, attended[sample * half : (sample + 1) * half]) for sample in range(2)
    ]
    attended = jnp.concatenate(attended, axis=0)
    attended = spread_columns(attended, order_ref[1])
    outward = (w_second[1, :, 3 * WIDTH - START - RIGHT :], w_second[2], w_second[3])
    projected = [jnp.dot(attended, part, preferred_element_type=jnp.float32) for part in outward]
    projected = jnp.concatenate(projected, axis=1)
    results = []
    for sample in range(2):
        state = x_ref[sample * half : (sample + 1) * half, :].astype(jnp.float32)
        state = state + mods_ref[sample, 2:3, :] * projected[sample * half : (sample + 1) * half]
        results.append(state.astype(jnp.bfloat16).astype(jnp.float32))
    cond, uncond = results
    guided = (uncond + 3.0 * (cond - uncond)).reshape(32, 8, WIDTH)
    for sample in range(2):
        both = jnp.concatenate([results[sample].reshape(32, 8, WIDTH), guided], axis=1)
        out_ref[sample * 32 : (sample + 1) * 32] = both.astype(jnp.bfloat16)


def kernel_call(body, out_shape, scratch, flops, moved, specs=None, limit=36, out_specs=None):
    return pl.pallas_call(
        body,
        **({} if specs is None else {"in_specs": specs}),
        **({} if out_specs is None else {"out_specs": out_specs}),
        out_shape=jax.tree.map(
            lambda shape: jax.ShapeDtypeStruct(shape, jnp.bfloat16),
            out_shape,
            is_leaf=lambda shape: isinstance(shape, tuple),
        ),
        scratch_shapes=scratch,
        cost_estimate=pl.CostEstimate(flops=flops, bytes_accessed=moved, transcendentals=0),
        compiler_params=pltpu.CompilerParams(vmem_limit_bytes=limit * 2**20),
    )


def along(block, axis, by):
    return lax.ppermute(block, axis, [(i, (i + by) % 4) for i in range(4)])


def along_z(block, by):
    def index(z):
        return z % 4 * 2 + z // 4

    return lax.ppermute(block, ("zl", "zh"), [(index(z), index((z + by) % 8)) for z in range(8)])


def other_core(block):
    return lax.ppermute(block, "c", [(0, 1), (1, 0)])


def gather_weights(w_qkv, w_out, prepared, mods):
    turn = lax.axis_index("y")
    later = jnp.concatenate([w_qkv[1], w_out[1]], axis=1)
    later_first = lax.dynamic_slice(later, (0, turn * LEFT), (SHARD, LEFT))
    later_second = lax.dynamic_slice(later, (0, START + turn * RIGHT), (SHARD, RIGHT))
    first = jnp.concatenate([w_qkv[0, :, :PAIR], later_first], axis=1)
    second = jnp.concatenate([w_qkv[0, :, PAIR:], w_out[0], later_second], axis=1)
    up, down, far = along(first, "x", 1), along(first, "x", 3), along(first, "x", 2)
    up_z, down_z = along_z(second, 1), along_z(second, 7)
    far_z = lax.ppermute(second, "zl", [(0, 2), (2, 0), (1, 3), (3, 1)])
    first = jnp.concatenate([first, down, far, up], axis=0)
    second = jnp.concatenate([second, down_z, far_z, up_z], axis=0)
    first, second, prepared = lax.optimization_barrier((first, second, prepared))
    near = [along_z(first, 1), along_z(first, 7), along(second, "x", 1), along(second, "x", 3)]
    own_other = [other_core(first), other_core(second)]
    first_far, second_far, near, mods = lax.optimization_barrier((first, second, near, mods))
    far = [along_z(first_far[:, :CUT], 2), along_z(first_far[:, CUT:], 6), along(second_far, "x", 2)]
    near_other = [other_core(block) for block in near]
    mine = [first] + near[:2] + far[:2] + [second] + near[2:] + far[2:]
    left = [block[:, PAIR:] for block in mine[:3]] + [mine[4][:, PAIR - CUT :]]
    right = [block[:, PAIR:] for block in mine[5:]]
    share = jnp.concatenate(
        [jnp.concatenate(left, axis=0), jnp.concatenate(right, axis=0)], axis=1
    )
    other = lax.ppermute(mods, "zh", [(0, 1), (1, 0)])
    leads = lax.axis_index("zh") == 0
    mods = jnp.stack([jnp.where(leads, mods, other), jnp.where(leads, other, mods)])
    share, mods = lax.optimization_barrier((share, mods))
    far_other = [other_core(block) for block in far]
    theirs = own_other[:1] + near_other[:2] + far_other[:2]
    theirs += own_other[1:] + near_other[2:] + far_other[2:]
    parts = [along(share, "y", by) for by in (1, 3, 2)]
    return mine + theirs, parts + [other_core(part) for part in parts], prepared, mods


def on_device(hidden, modulation, w_qkv, w_out):
    state = hidden.reshape(PATCHES, WIDTH)
    mods = modulation[0]

    prepared = kernel_call(prepare_kernel, [(PATCHES, WIDTH)] * 2, [], 10**9, 10**7)(state, mods[0])
    weights, later, (first, second), both_mods = gather_weights(w_qkv, w_out, prepared, mods[1])
    layer_one, kept_first, kept_second = kernel_call(
        spatial_kernel,
        [(ROWS, WIDTH), (WIDTH, LEFT), (WIDTH, RIGHT)],
        [
            pltpu.VMEM((WIDTH, PAIR), jnp.bfloat16),
            pltpu.VMEM((WIDTH, PAIR), jnp.bfloat16),
            pltpu.VMEM((WIDTH, LEFT), jnp.bfloat16),
            pltpu.VMEM((WIDTH, RIGHT), jnp.bfloat16),
            pltpu.VMEM((WIDTH, WIDTH), jnp.bfloat16),
            pltpu.VMEM((PATCHES, 3 * WIDTH), jnp.bfloat16),
            pltpu.VMEM((PATCHES, WIDTH), jnp.float32),
            pltpu.SemaphoreType.DMA((36,)),
        ],
        10**10,
        2 * 10**7,
        [pl.BlockSpec(memory_space=pltpu.VMEM)] * 4 + [pl.BlockSpec(memory_space=pl.ANY)] * 18,
        38,
        [pl.BlockSpec(memory_space=pltpu.VMEM)] + [pl.BlockSpec(memory_space=pltpu.HBM)] * 2,
    )(first, second, state, mods[0], *weights)
    late_mods, _ = lax.optimization_barrier((both_mods, later[0]))
    by_x, by_z = kernel_call(order_kernel, [(WIDTH, WIDTH)] * 2, [], 10**9, 10**7)(late_mods)
    by_patch = lax.all_to_all(layer_one.reshape(64, 8, WIDTH), PAIRED, 0, 0, tiled=True)
    result = kernel_call(
        temporal_kernel,
        (64, 16, WIDTH),
        [
            pltpu.VMEM((4, WIDTH, LEFT), jnp.bfloat16),
            pltpu.VMEM((4, WIDTH, RIGHT), jnp.bfloat16),
            pltpu.VMEM((2, WIDTH, WIDTH), jnp.bfloat16),
            pltpu.VMEM((ROWS, WIDTH), jnp.bfloat16),
            pltpu.VMEM((ROWS, WIDTH), jnp.bfloat16),
            pltpu.VMEM((ROWS, 3 * WIDTH), jnp.bfloat16),
            pltpu.VMEM((ROWS, WIDTH), jnp.float32),
            pltpu.SemaphoreType.DMA((52,)),
        ],
        10**10,
        2 * 10**7,
        [pl.BlockSpec(memory_space=pltpu.VMEM)] * 2 + [pl.BlockSpec(memory_space=pltpu.HBM)] * 10,
        58,
    )(by_patch.reshape(ROWS, WIDTH), both_mods, kept_first, kept_second, *later, by_x, by_z)
    by_frame = lax.all_to_all(result, PAIRED, 0, 0, tiled=True)
    hidden_out = by_frame[:, :8].reshape(ROWS, WIDTH)[:PATCHES]
    guided = by_frame[:, 8:].reshape(ROWS, WIDTH)[:PATCHES]
    return hidden_out.reshape(hidden.shape), guided.reshape(hidden.shape)


def solution(mesh):
    split = Mesh(mesh.devices.reshape(4, 4, 2, 4, 2), ("x", "zl", "c", "y", "zh"))
    batch, seq = ("y", "zh"), SEQ
    placed = (
        P(batch, seq, None, None),
        P(batch, None, None, None),
        P(None, seq, None),
        P(None, seq, None),
    )
    return jax.shard_map(
        on_device,
        mesh=split,
        in_specs=placed,
        out_specs=(P(batch, seq, None, None), P(batch, seq, None, None)),
        check_vma=False,
    )
```
